512 devices in a mesh: tok: 16 (over z_lo, core), exp: 32 (over z_hi, x, y).
Axes of the slice: x: 4, y: 4, z: 16 (z_hi: 2, z_lo: 8; z = z_hi * 8 + z_lo), core: 2. Of those that a mesh axis runs over, the one named last changes fastest.
Arguments:
- patches: bfloat16 [4096, 1280], P('tok', 'exp'), may hold values from -30 to 30
- router: bfloat16 [128, 1280], P('exp'), may hold values from -150 to 150
- w_in: bfloat16 [32, 5120, 1280], P('exp', 'tok'), may hold values from -0.15625 to 0.15625
- w_out: bfloat16 [32, 5120, 1280], P('exp', 'tok'), may hold values from -0.078125 to 0.078125
- grad_mixed: bfloat16 [4096, 1280], P('tok', 'exp'), may hold values from -6 to 6
Outputs:
- mixed: bfloat16 [4096, 1280], P(('tok', 'exp'))
- grad_patches: bfloat16 [4096, 1280], P(('tok', 'exp'))
- grad_router: bfloat16 [128, 1280], P('exp')
- grad_w_in: bfloat16 [32, 5120, 1280], P('exp', 'tok')
- grad_w_out: bfloat16 [32, 5120, 1280], P('exp', 'tok')
The draws below stay inside these ranges and needn't reach their ends.
All inputs are finite; a program needn't handle non-finite values.
Results may differ from the reference program's by a relative error of at most 0.035.
Values may be sent and summed in bfloat16 or wider, within the bound.
No kernel may reach another device: no remote copies, remote signals or barrier semaphores. Data moves between devices by JAX's collectives and lax.ppermute only.
A program may use at most 64 MiB of HBM per device.

```python
import math
import jax
import jax.numpy as jnp
from jax import lax

D = 1280
FF = 5120
SLOTS_PER = 4
EXPERTS = 32
SLOTS = 128
TOKENS = 4096


def joint_draw(key):
    sub_keys = jax.random.split(key, 7)
    patch_normal = jnp.clip(jax.random.normal(sub_keys[0], (TOKENS, D), jnp.float32), -4.0, 4.0)
    patch_rows = jnp.exp(jax.random.uniform(sub_keys[2], (TOKENS, 1), jnp.float32, math.log(0.4), math.log(4.0)))
    patch_rise = 0.7 + 0.6 * jnp.arange(TOKENS, dtype=jnp.float32)[:, None] / TOKENS
    patches = patch_normal * patch_rows * patch_rise
    slot_normal = jnp.clip(jax.random.normal(sub_keys[4], (SLOTS, D), jnp.float32), -4.0, 4.0)
    slot_rows = jnp.exp(jax.random.uniform(sub_keys[6], (SLOTS, 1), jnp.float32, math.log(0.3), math.log(3.0)))
    slot_rise = 0.7 + 0.6 * jnp.arange(SLOTS, dtype=jnp.float32)[:, None] / SLOTS
    router = 0.5 * slot_normal * slot_rows * slot_rise
    return (patches, router)


def draw_patches(key, part):
    drawn = joint_draw(key)
    return drawn[0].astype(jnp.bfloat16)


def draw_router(key, part):
    drawn = joint_draw(key)
    return drawn[1].astype(jnp.bfloat16)


def steps_of(rng, dims, shards, smallest, high):
    def one(axis_at, shards_of):
        draws = jax.random.uniform(jax.random.fold_in(jax.random.fold_in(rng, 6), axis_at), (shards_of,), jnp.float32, smallest / len(shards), high / len(shards))
        return jnp.repeat(jnp.exp(draws), dims[axis_at] // shards_of).reshape((-1,) + (1,) * (len(dims) - axis_at - 1))

    level = one(*shards[0])
    for cut in shards[1:]:
        level = level * one(*cut)
    return level


def scatter_about(rng, extent, width, bound, pieces=(), kind=jnp.bfloat16):
    array = width * jax.random.normal(rng, extent, jnp.float32)
    if pieces:
        array = array * steps_of(rng, extent, pieces, -0.22, 0.18)
    return jnp.clip(array, -bound, bound).astype(kind)


def setup_inputs(seed: int = 0) -> dict:
    arg_keys = jax.random.split(jax.random.key(seed), 6)
    patches = draw_patches(jax.random.fold_in(arg_keys[5], 71), 0)
    router = draw_router(jax.random.fold_in(arg_keys[5], 71), 0)
    w_in = scatter_about(arg_keys[2], (EXPERTS, FF, D), D ** -0.5, 0.15625, ((0, 32), (1, 16)))
    w_out = scatter_about(arg_keys[3], (EXPERTS, FF, D), FF ** -0.5, 0.078125, ((0, 32), (1, 16)))
    grad_mixed = scatter_about(arg_keys[4], (TOKENS, D), 1.0, 6.0, ((0, 16), (1, 32)))
    return {"patches": patches, "router": router, "w_in": w_in, "w_out": w_out, "grad_mixed": grad_mixed}


tanh_coef = 0.7978845608028654
cubic_coef = 0.044715

def gelu_value(inputs):
    return jax.nn.gelu(inputs, approximate=True)

def gelu_slope(inputs):
    inner = tanh_coef * (inputs + cubic_coef * inputs * inputs * inputs)
    hyper = jnp.tanh(inner)
    return 0.5 * (1.0 + hyper) + 0.5 * inputs * (1.0 - hyper * hyper) * tanh_coef * (1.0 + 3.0 * cubic_coef * inputs * inputs)

def reference(patches, router, w_in, w_out, grad_mixed):
    score_scale = 1.0 / math.sqrt(D)
    logits = jnp.dot(router, patches.T, preferred_element_type=jnp.float32) * score_scale
    disp_prob = jax.nn.softmax(logits, axis=1)
    comb_prob = jax.nn.softmax(logits, axis=0)
    dispatch = disp_prob.astype(jnp.bfloat16)
    combine = comb_prob.astype(jnp.bfloat16)
    slot_in = jnp.dot(dispatch, patches, preferred_element_type=jnp.float32).astype(jnp.bfloat16)
    expert_in = slot_in.reshape(EXPERTS, SLOTS_PER, D)

    def forward_expert(operands):
        block_in, weight_in, weight_out = operands
        pre_act = jnp.dot(block_in, weight_in.T, preferred_element_type=jnp.float32)
        hidden = gelu_value(pre_act).astype(jnp.bfloat16)
        return (pre_act, hidden, jnp.dot(hidden, weight_out, preferred_element_type=jnp.float32))
    pre_act, hidden, expert_out = lax.map(forward_expert, (expert_in, w_in, w_out))
    slot_out = expert_out.reshape(SLOTS, D).astype(jnp.bfloat16)
    mixed = jnp.dot(combine.T, slot_out, preferred_element_type=jnp.float32).astype(jnp.bfloat16)
    grad_comb = jnp.dot(slot_out, grad_mixed.T, preferred_element_type=jnp.float32)
    grad_slot_out = jnp.dot(combine, grad_mixed, preferred_element_type=jnp.float32).astype(jnp.bfloat16)

    def backward_expert(operands):
        block_in, pre_block, hidden_block, grad_block, weight_in, weight_out = operands
        grad_weight_out = jnp.dot(hidden_block.T, grad_block, preferred_element_type=jnp.float32).astype(jnp.bfloat16)
        grad_hidden = jnp.dot(grad_block, weight_out.T, preferred_element_type=jnp.float32)
        grad_pre = (grad_hidden * gelu_slope(pre_block)).astype(jnp.bfloat16)
        grad_weight_in = jnp.dot(grad_pre.T, block_in, preferred_element_type=jnp.float32).astype(jnp.bfloat16)
        return (grad_weight_in, grad_weight_out, jnp.dot(grad_pre, weight_in, preferred_element_type=jnp.float32))
    grad_w_in, grad_w_out, expert_grad = lax.map(backward_expert, (expert_in, pre_act, hidden, grad_slot_out.reshape(EXPERTS, SLOTS_PER, D), w_in, w_out))
    grad_slot_in = expert_grad.reshape(SLOTS, D).astype(jnp.bfloat16)
    grad_disp = jnp.dot(grad_slot_in, patches.T, preferred_element_type=jnp.float32)
    slot_dot = lax.optimization_barrier(jnp.sum(disp_prob * grad_disp, axis=1, keepdims=True))
    patch_dot = lax.optimization_barrier(jnp.sum(comb_prob * grad_comb, axis=0, keepdims=True))
    grad_logits = disp_prob * (grad_disp - slot_dot) + comb_prob * (grad_comb - patch_dot)
    scaled = (grad_logits * score_scale).astype(jnp.bfloat16)
    grad_router = jnp.dot(scaled, patches, preferred_element_type=jnp.float32).astype(jnp.bfloat16)
    grad_patches = (jnp.dot(dispatch.T, grad_slot_in, preferred_element_type=jnp.float32) + jnp.dot(scaled.T, router, preferred_element_type=jnp.float32)).astype(jnp.bfloat16)
    return (mixed, grad_patches, grad_router, grad_w_in, grad_w_out)
```

```python
import math

import jax
import jax.numpy as jnp
from jax import lax
from jax.sharding import Mesh, PartitionSpec as P

tanh_coef = 0.7978845608028654
cubic_coef = 0.044715
f32 = jnp.float32
bf16 = jnp.bfloat16
swap = [(0, 1), (1, 0)]


def gelu_value(inputs):
    return jax.nn.gelu(inputs, approximate=True)


def gelu_slope(inputs):
    inner = tanh_coef * (inputs + cubic_coef * inputs * inputs * inputs)
    hyper = jnp.tanh(inner)
    return 0.5 * (1.0 + hyper) + 0.5 * inputs * (1.0 - hyper * hyper) * tanh_coef * (
        1.0 + 3.0 * cubic_coef * inputs * inputs
    )


def contract(left, right, left_dim, right_dim):
    return lax.dot_general(
        left, right, (((left_dim,), (right_dim,)), ((), ())), preferred_element_type=f32
    )


def split(value, terms):
    out = []
    for _ in range(terms):
        head = lax.reduce_precision(value, 8, 7)
        out.append(head.astype(bf16))
        value = value - head
    return out


def spread(block, axes, count):
    return lax.all_to_all(
        jnp.broadcast_to(block[None], (count,) + block.shape), axes, 0, 0, tiled=True
    )


def body(patches, router, w_in, w_out, grad_mixed):
    core = lax.axis_index("core")
    expert = lax.axis_index(("zh", "x", "y"))
    low = core == 0
    width = router.shape[1]
    half = width // 2
    scale = 1.0 / math.sqrt(width)

    def mine(array):
        return jnp.where(low, array[:, :half], array[:, half:])

    def other(array):
        return jnp.where(low, array[:, half:], array[:, :half])

    def whole(own, got):
        return jnp.concatenate([jnp.where(low, own, got), jnp.where(low, got, own)], axis=1)

    rows = router.reshape(4, 5, 256).transpose(1, 0, 2).reshape(20, 256)
    packed = jnp.concatenate([patches.T, grad_mixed.T, rows], axis=0)
    got = spread(packed, ("zh", "x", "y"), 32)
    patches_t = got[:, :40].reshape(width, 256)
    cotangent_t = got[:, 40:80].reshape(width, 256)
    router_all = got[:, 80:].reshape(32, 5, 4, 256).transpose(0, 2, 1, 3).reshape(128, width)

    logits = contract(router_all, patches_t, 1, 0) * scale
    comb_exp = jnp.exp(logits - jnp.max(logits, axis=0, keepdims=True))
    comb_prob = comb_exp / jnp.sum(comb_exp, axis=0, keepdims=True)
    combine = comb_prob.astype(bf16)
    top = jnp.max(logits, axis=1)
    disp_exp = jnp.exp(logits - top[:, None])
    total = jnp.sum(disp_exp, axis=1)

    own_exp = lax.dynamic_slice_in_dim(disp_exp, 4 * expert, 4, 0)
    own_comb = lax.dynamic_slice_in_dim(combine, 4 * expert, 4, 0)
    slot_part = contract(jnp.concatenate(split(own_exp, 3), axis=0), patches_t, 1, 1)
    slot_part = slot_part[0:4] + slot_part[4:8] + slot_part[8:12]
    grad_part = contract(own_comb, cotangent_t, 1, 1)

    both = jnp.concatenate([slot_part, grad_part], axis=0)
    stats = jnp.concatenate([top[None], total[None], jnp.zeros((6, 128), f32)], axis=0)
    got = lax.ppermute(jnp.concatenate([other(both), stats], axis=1), "core", swap)
    top_b, total_b = got[0, half:], got[1, half:]
    top_ab = jnp.maximum(top, top_b)
    scale_a, scale_b = jnp.exp(top - top_ab), jnp.exp(top_b - top_ab)
    total = total * scale_a + total_b * scale_b

    def own(vector):
        return lax.dynamic_slice_in_dim(vector, 4 * expert, 4, vector.ndim - 1)

    both = mine(both)
    both = jnp.concatenate(
        [
            both[:4] * own(scale_a)[:, None] + got[:4, :half] * own(scale_b)[:, None],
            both[4:] + got[4:, :half],
        ],
        axis=0,
    )
    stats = jnp.concatenate([top_ab[None], total[None], jnp.zeros((6, 128), f32)], axis=0)
    got = spread(jnp.concatenate([both, stats], axis=1), "zl", 8)
    tops = got[:, 0, half:]
    slot_top = jnp.max(tops, axis=0)
    scales = jnp.exp(tops - slot_top)
    slot_sum = jnp.sum(got[:, 1, half:] * scales, axis=0)
    slot_half = jnp.sum(got[:, :4, :half] * own(scales)[:, :, None], axis=0) / own(slot_sum)[:, None]
    grad_half = jnp.sum(got[:, 4:, :half], axis=0)
    halves = jnp.concatenate([slot_half, grad_half], axis=0).astype(bf16)
    halves = whole(halves, lax.ppermute(halves, "core", swap))
    slot_in, grad_slot_out = halves[:4], halves[4:]

    pre_act = contract(slot_in, w_in[0], 1, 1)
    hidden = gelu_value(pre_act).astype(bf16)
    grad_hidden = contract(grad_slot_out, w_out[0], 1, 1)
    grad_pre = (grad_hidden * gelu_slope(pre_act)).astype(bf16)
    out_part = contract(hidden, w_out[0], 1, 0)
    grad_in_part = contract(grad_pre, w_in[0], 1, 0)
    grad_w_out = contract(hidden, grad_slot_out, 0, 0).astype(bf16)[None]
    grad_w_in = contract(grad_pre, slot_in, 0, 0).astype(bf16)[None]

    parts = jnp.concatenate([out_part, grad_in_part], axis=0)
    parts = mine(parts) + lax.ppermute(other(parts), "core", swap)
    block = jnp.concatenate([parts.astype(bf16)] + split(slot_half, 2), axis=0)
    got = spread(block, ("zh", "zl"), 16).reshape(2, 8, 16, half)
    sums = jnp.sum(got[:, :, :8].astype(f32), axis=1).astype(bf16)
    slot_pair = got[:, 0, 8:12].astype(f32) + got[:, 0, 12:].astype(f32)
    dots = jnp.sum(sums[:, 4:].astype(f32) * slot_pair, axis=2)
    dots = jnp.stack(split(dots, 3), axis=-1)
    dots = jnp.pad(dots, ((0, 0), (4, 0), (0, 125)))
    block = jnp.concatenate([sums, dots], axis=2).reshape(16, half + 128)
    got = spread(block, ("x", "y"), 16).reshape(16, 2, 2, 4, half + 128)
    got = got.transpose(2, 1, 0, 3, 4).reshape(256, half + 128)
    back = lax.ppermute(got, "core", swap)
    rows = whole(got[:, :half], back[:, :half])
    slot_out, grad_slot_in = rows[:128], rows[128:]
    slot_dot = jnp.sum(
        got[128:, half : half + 3].astype(f32) + back[128:, half : half + 3].astype(f32),
        axis=1,
    )

    disp_prob = jnp.exp(logits - slot_top[:, None]) / slot_sum[:, None]
    dispatch = disp_prob.astype(bf16)
    grad_comb = contract(slot_out, cotangent_t, 1, 0)
    grad_disp = contract(grad_slot_in, patches_t, 1, 0)
    patch_dot = jnp.sum(comb_prob * grad_comb, axis=0)
    grad_logits = disp_prob * (grad_disp - slot_dot[:, None]) + comb_prob * (
        grad_comb - patch_dot[None, :]
    )
    scaled = (grad_logits * scale).astype(bf16)

    own_scaled = lax.dynamic_slice_in_dim(scaled, 4 * expert, 4, 0)
    router_part = contract(own_scaled, patches_t, 1, 1).astype(bf16)
    got = spread(router_part.reshape(8, half), ("zl", "core"), 16)
    grad_router = jnp.sum(got.astype(f32), axis=0).astype(bf16).reshape(4, width)

    def tokens(array):
        return lax.dynamic_slice_in_dim(array, 8 * expert, 8, 1)

    mixed = contract(tokens(combine), slot_out, 0, 0).astype(bf16)
    grad_patches = contract(tokens(dispatch), grad_slot_in, 0, 0) + contract(
        tokens(scaled), router_all, 0, 0
    )
    return (mixed, grad_patches.astype(bf16), grad_router, grad_w_in, grad_w_out)


def solution(mesh):
    fine = Mesh(mesh.devices.reshape(8, 2, 2, 4, 4), ("zl", "core", "zh", "x", "y"))
    tok, exp = ("zl", "core"), ("zh", "x", "y")
    return jax.shard_map(
        body,
        mesh=fine,
        in_specs=(
            P(tok, exp),
            P(exp, None),
            P(exp, tok, None),
            P(exp, tok, None),
            P(tok, exp),
        ),
        out_specs=(
            P(tok + exp, None),
            P(tok + exp, None),
            P(exp, None),
            P(exp, tok, None),
            P(exp, tok, None),
        ),
        check_vma=False,
    )
```

```python
import math

import jax
import jax.numpy as jnp
from jax import lax
from jax.sharding import Mesh, PartitionSpec as P

tanh_coef = 0.7978845608028654
cubic_coef = 0.044715
f32 = jnp.float32
bf16 = jnp.bfloat16
swap = [(0, 1), (1, 0)]


def gelu_value(inputs):
    return jax.nn.gelu(inputs, approximate=True)


def gelu_slope(inputs):
    inner = tanh_coef * (inputs + cubic_coef * inputs * inputs * inputs)
    hyper = jnp.tanh(inner)
    return 0.5 * (1.0 + hyper) + 0.5 * inputs * (1.0 - hyper * hyper) * tanh_coef * (
        1.0 + 3.0 * cubic_coef * inputs * inputs
    )


def contract(left, right, left_dim, right_dim):
    return lax.dot_general(
        left, right, (((left_dim,), (right_dim,)), ((), ())), preferred_element_type=f32
    )


def split(value, terms):
    out = []
    for _ in range(terms):
        head = lax.reduce_precision(value, 8, 7)
        out.append(head.astype(bf16))
        value = value - head
    return out


def spread(block, axes, count):
    return lax.all_to_all(
        jnp.broadcast_to(block[None], (count,) + block.shape), axes, 0, 0, tiled=True
    )


def body(patches, router, w_in, w_out, grad_mixed):
    core = lax.axis_index("core")
    expert = lax.axis_index(("zh", "x", "y"))
    low = core == 0
    width = router.shape[1]
    half = width // 2
    scale = 1.0 / math.sqrt(width)

    def mine(array):
        return jnp.where(low, array[:, :half], array[:, half:])

    def other(array):
        return jnp.where(low, array[:, half:], array[:, :half])

    def whole(own, got):
        return jnp.concatenate([jnp.where(low, own, got), jnp.where(low, got, own)], axis=1)

    rows = router.reshape(4, 5, 256).transpose(1, 0, 2).reshape(20, 256)
    packed = jnp.concatenate([patches.T, grad_mixed.T, rows], axis=0)
    partner = lax.ppermute(packed, "zh", swap)
    first = lax.axis_index("zh") == 0
    pair = jnp.stack([jnp.where(first, packed, partner), jnp.where(first, partner, packed)])
    got = spread(pair, ("x", "y"), 16)
    patches_t = got[:, :, :40].transpose(1, 0, 2, 3).reshape(width, 256)
    cotangent_t = got[:, :, 40:80].transpose(1, 0, 2, 3).reshape(width, 256)
    router_all = (
        got[:, :, 80:].reshape(16, 2, 5, 4, 256).transpose(1, 0, 3, 2, 4).reshape(128, width)
    )

    logits = contract(router_all, patches_t, 1, 0) * scale
    comb_exp = jnp.exp(logits - jnp.max(logits, axis=0, keepdims=True))
    comb_prob = comb_exp / jnp.sum(comb_exp, axis=0, keepdims=True)
    combine = comb_prob.astype(bf16)
    top = jnp.max(logits, axis=1)
    disp_exp = jnp.exp(logits - top[:, None])
    total = jnp.sum(disp_exp, axis=1)

    own_exp = lax.dynamic_slice_in_dim(disp_exp, 4 * expert, 4, 0)
    own_comb = lax.dynamic_slice_in_dim(combine, 4 * expert, 4, 0)
    slot_part = contract(jnp.concatenate(split(own_exp, 3), axis=0), patches_t, 1, 1)
    slot_part = slot_part[0:4] + slot_part[4:8] + slot_part[8:12]
    grad_part = contract(own_comb, cotangent_t, 1, 1)

    both = jnp.concatenate([slot_part, grad_part], axis=0)
    stats = jnp.concatenate([top[None], total[None], jnp.zeros((6, 128), f32)], axis=0)
    got = lax.ppermute(jnp.concatenate([other(both), stats], axis=1), "core", swap)
    top_b, total_b = got[0, half:], got[1, half:]
    top_ab = jnp.maximum(top, top_b)
    scale_a, scale_b = jnp.exp(top - top_ab), jnp.exp(top_b - top_ab)
    total = total * scale_a + total_b * scale_b

    def own(vector):
        return lax.dynamic_slice_in_dim(vector, 4 * expert, 4, vector.ndim - 1)

    both = mine(both)
    both = jnp.concatenate(
        [
            both[:4] * own(scale_a)[:, None] + got[:4, :half] * own(scale_b)[:, None],
            both[4:] + got[4:, :half],
        ],
        axis=0,
    )
    stats = jnp.concatenate([top_ab[None], total[None], jnp.zeros((6, 128), f32)], axis=0)
    got = spread(jnp.concatenate([both, stats], axis=1), "zl", 8)
    tops = got[:, 0, half:]
    slot_top = jnp.max(tops, axis=0)
    scales = jnp.exp(tops - slot_top)
    slot_sum = jnp.sum(got[:, 1, half:] * scales, axis=0)
    slot_half = jnp.sum(got[:, :4, :half] * own(scales)[:, :, None], axis=0) / own(slot_sum)[:, None]
    grad_half = jnp.sum(got[:, 4:, :half], axis=0)
    halves = jnp.concatenate([slot_half, grad_half], axis=0).astype(bf16)
    halves = whole(halves, lax.ppermute(halves, "core", swap))
    slot_in, grad_slot_out = halves[:4], halves[4:]

    pre_act = contract(slot_in, w_in[0], 1, 1)
    hidden = gelu_value(pre_act).astype(bf16)
    grad_hidden = contract(grad_slot_out, w_out[0], 1, 1)
    grad_pre = (grad_hidden * gelu_slope(pre_act)).astype(bf16)
    out_part = contract(hidden, w_out[0], 1, 0)
    grad_in_part = contract(grad_pre, w_in[0], 1, 0)
    grad_w_out = contract(hidden, grad_slot_out, 0, 0).astype(bf16)[None]
    grad_w_in = contract(grad_pre, slot_in, 0, 0).astype(bf16)[None]

    parts = jnp.concatenate([out_part, grad_in_part], axis=0)
    parts = mine(parts) + lax.ppermute(other(parts), "core", swap)
    piece = lax.dynamic_slice_in_dim(
        jnp.concatenate(split(slot_half, 2), axis=0), lax.axis_index("zl"), 1, 0
    )
    piece = jnp.pad(piece.reshape(5, 128), ((0, 3), (0, 0)))
    block = jnp.concatenate([parts.astype(bf16), piece], axis=1)
    got = spread(block, ("zh", "zl"), 16).reshape(2, 8, 8, half + 128)
    sums = jnp.sum(got[..., :half].astype(f32), axis=1).astype(bf16)
    pieces = got[:, :, :5, half:].reshape(2, 2, 4, half).astype(f32)
    slot_pair = pieces[:, 0] + pieces[:, 1]
    dots = jnp.sum(sums[:, 4:].astype(f32) * slot_pair, axis=2)
    dots = jnp.stack(split(dots, 3), axis=-1)
    dots = jnp.pad(dots, ((0, 0), (4, 0), (0, 125)))
    block = jnp.concatenate([sums, dots], axis=2).reshape(16, half + 128)
    got = spread(block, ("x", "y"), 16).reshape(16, 2, 2, 4, half + 128)
    got = got.transpose(2, 1, 0, 3, 4).reshape(256, half + 128)
    back = lax.ppermute(got, "core", swap)
    rows = whole(got[:, :half], back[:, :half])
    slot_out, grad_slot_in = rows[:128], rows[128:]
    slot_dot = jnp.sum(
        got[128:, half : half + 3].astype(f32) + back[128:, half : half + 3].astype(f32),
        axis=1,
    )

    disp_prob = jnp.exp(logits - slot_top[:, None]) / slot_sum[:, None]
    dispatch = disp_prob.astype(bf16)
    grad_comb = contract(slot_out, cotangent_t, 1, 0)
    grad_disp = contract(grad_slot_in, patches_t, 1, 0)
    patch_dot = jnp.sum(comb_prob * grad_comb, axis=0)
    grad_logits = disp_prob * (grad_disp - slot_dot[:, None]) + comb_prob * (
        grad_comb - patch_dot[None, :]
    )
    scaled = (grad_logits * scale).astype(bf16)

    own_scaled = lax.dynamic_slice_in_dim(scaled, 4 * expert, 4, 0)
    router_part = contract(own_scaled, patches_t, 1, 1).astype(bf16)
    got = spread(router_part.reshape(8, half), ("zl", "core"), 16)
    grad_router = jnp.sum(got.astype(f32), axis=0).astype(bf16).reshape(4, width)

    def tokens(array):
        return lax.dynamic_slice_in_dim(array, 8 * expert, 8, 1)

    mixed = contract(tokens(combine), slot_out, 0, 0).astype(bf16)
    grad_patches = contract(tokens(dispatch), grad_slot_in, 0, 0) + contract(
        tokens(scaled), router_all, 0, 0
    )
    return (mixed, grad_patches.astype(bf16), grad_router, grad_w_in, grad_w_out)


def solution(mesh):
    fine = Mesh(mesh.devices.reshape(8, 2, 2, 4, 4), ("zl", "core", "zh", "x", "y"))
    tok, exp = ("zl", "core"), ("zh", "x", "y")
    return jax.shard_map(
        body,
        mesh=fine,
        in_specs=(
            P(tok, exp),
            P(exp, None),
            P(exp, tok, None),
            P(exp, tok, None),
            P(tok, exp),
        ),
        out_specs=(
            P(tok + exp, None),
            P(tok + exp, None),
            P(exp, None),
            P(exp, tok, None),
            P(exp, tok, None),
        ),
        check_vma=False,
    )
```

```python
import math

import jax
import jax.numpy as jnp
from jax import lax
from jax.experimental import pallas as pl
from jax.experimental.pallas import tpu as pltpu
from jax.sharding import Mesh, PartitionSpec as P

tanh_coef = 0.7978845608028654
cubic_coef = 0.044715
f32 = jnp.float32
bf16 = jnp.bfloat16
swap = [(0, 1), (1, 0)]


def gelu_value(inputs):
    return jax.nn.gelu(inputs, approximate=True)


def gelu_slope(inputs):
    inner = tanh_coef * (inputs + cubic_coef * inputs * inputs * inputs)
    hyper = jnp.tanh(inner)
    return 0.5 * (1.0 + hyper) + 0.5 * inputs * (1.0 - hyper * hyper) * tanh_coef * (
        1.0 + 3.0 * cubic_coef * inputs * inputs
    )


def contract(left, right, left_dim, right_dim):
    return lax.dot_general(
        left, right, (((left_dim,), (right_dim,)), ((), ())), preferred_element_type=f32
    )


def split(value, terms):
    out = []
    for _ in range(terms):
        head = lax.reduce_precision(value, 8, 7)
        out.append(head.astype(bf16))
        value = value - head
    return out


def spread(block, axes, count):
    return lax.all_to_all(
        jnp.broadcast_to(block[None], (count,) + block.shape), axes, 0, 0, tiled=True
    )


def fan_kernel(block_ref, out_ref):
    for peer in range(out_ref.shape[0]):
        out_ref[peer] = block_ref[...]


def fan(block, count, flops):
    return pl.pallas_call(
        fan_kernel,
        out_shape=jax.ShapeDtypeStruct((count,) + block.shape, block.dtype),
        in_specs=[pl.BlockSpec(memory_space=pltpu.VMEM)],
        out_specs=pl.BlockSpec(memory_space=pltpu.VMEM),
        compiler_params=pltpu.CompilerParams(vmem_limit_bytes=16 << 20),
        cost_estimate=pl.CostEstimate(flops=flops, bytes_accessed=0, transcendentals=0),
    )(block)


def body(patches, router, w_in, w_out, grad_mixed):
    core = lax.axis_index("core")
    expert = lax.axis_index(("zh", "x", "y"))
    low = core == 0
    width = router.shape[1]
    half = width // 2
    scale = 1.0 / math.sqrt(width)

    def mine(array):
        return jnp.where(low, array[:, :half], array[:, half:])

    def other(array):
        return jnp.where(low, array[:, half:], array[:, :half])

    def whole(own, got):
        return jnp.concatenate([jnp.where(low, own, got), jnp.where(low, got, own)], axis=1)

    packed = jnp.concatenate(
        [patches.T, grad_mixed.T] + [router[:, k * 256 : k * 256 + 256] for k in range(5)], axis=0
    )
    first = lax.axis_index("zh") == 0
    far = lax.all_to_all(fan(lax.ppermute(packed, "zh", swap), 16, 10**11), ("x", "y"), 0, 0, tiled=True)
    near = spread(packed, ("x", "y"), 16)

    def ordered(start, stop):
        own, partner = near[:, start:stop], far[:, start:stop]
        return jnp.stack([jnp.where(first, own, partner), jnp.where(first, partner, own)])

    patches_t = ordered(0, 40).reshape(width, 256)
    cotangent_t = ordered(40, 80).reshape(width, 256)
    router_all = (
        ordered(80, 100).reshape(32, 5, 4, 256).transpose(0, 2, 1, 3).reshape(128, width)
    )

    logits = contract(router_all, patches_t, 1, 0) * scale
    comb_exp = jnp.exp(logits - jnp.max(logits, axis=0, keepdims=True))
    comb_prob = comb_exp / jnp.sum(comb_exp, axis=0, keepdims=True)
    combine = comb_prob.astype(bf16)
    top = jnp.max(logits, axis=1)
    total = jnp.sum(jnp.exp(logits - top[:, None]), axis=1)

    stats = jnp.stack(split(top, 3) + split(total, 3))
    got = spread(jnp.pad(stats, ((0, 2), (0, 0))), ("zl", "core"), 16).astype(f32)
    tops = got[:, 0] + got[:, 1] + got[:, 2]
    slot_top = jnp.max(tops, axis=0)
    slot_sum = jnp.sum((got[:, 3] + got[:, 4] + got[:, 5]) * jnp.exp(tops - slot_top), axis=0)
    disp_prob = jnp.exp(logits - slot_top[:, None]) / slot_sum[:, None]
    dispatch, rest = split(disp_prob, 2)

    def own(array):
        return lax.dynamic_slice_in_dim(array, 4 * expert, 4, 0)

    parts = jnp.concatenate(
        [
            contract(jnp.concatenate([own(dispatch), own(rest)], axis=0), patches_t, 1, 1),
            contract(own(combine), cotangent_t, 1, 1),
        ],
        axis=0,
    )
    parts = mine(parts) + lax.ppermute(other(parts), "core", swap)
    block = jnp.concatenate(
        split(parts[:4], 2) + [parts[4:8].astype(bf16)] + split(parts[8:], 2), axis=0
    )
    got = jnp.sum(spread(block, "zl", 8).astype(f32), axis=0)
    slot_half = got[:4] + got[4:8]
    grad_half = got[12:16] + got[16:]
    halves = jnp.concatenate([slot_half, grad_half], axis=0).astype(bf16)

    rows = w_in.shape[1]
    pair_in = jnp.concatenate([mine(w_in[0]), lax.ppermute(other(w_in[0]), "core", swap)], axis=0)
    pair_out = jnp.concatenate(
        [mine(w_out[0]), lax.ppermute(other(w_out[0]), "core", swap)], axis=0
    )
    pre = jnp.concatenate(
        [contract(halves[:4], pair_in, 1, 1), contract(halves[4:], pair_out, 1, 1)], axis=0
    )
    pre = pre + lax.ppermute(
        jnp.concatenate([pre[:, rows:], pre[:, :rows]], axis=1), "core", swap
    )
    pre_act, grad_hidden = pre[:4], pre[4:]
    hidden = gelu_value(pre_act).astype(bf16)
    grad_pre = (grad_hidden * gelu_slope(pre_act)).astype(bf16)
    parts = jnp.concatenate(
        [contract(hidden, pair_out, 1, 0), contract(grad_pre, pair_in, 1, 0)], axis=0
    )
    full = whole(halves, lax.ppermute(halves, "core", swap))
    grad_w_out = contract(hidden[:, :rows], full[4:], 0, 0).astype(bf16)[None]
    grad_w_in = contract(grad_pre[:, :rows], full[:4], 0, 0).astype(bf16)[None]

    piece = lax.dynamic_slice_in_dim(
        jnp.concatenate(split(slot_half + got[8:12], 2), axis=0), lax.axis_index("zl"), 1, 0
    )
    piece = jnp.pad(piece.reshape(5, 128), ((0, 3), (0, 0)))
    block = jnp.concatenate(split(parts, 2) + [piece], axis=1)
    got = spread(block, ("zh", "zl"), 16).reshape(2, 8, 8, width + 128)
    sums = jnp.sum(got[..., :width].astype(f32), axis=1)
    sums = (sums[..., :half] + sums[..., half:]).astype(bf16)
    pieces = got[:, :, :5, width:].reshape(2, 2, 4, half).astype(f32)
    slot_pair = pieces[:, 0] + pieces[:, 1]
    dots = jnp.sum(sums[:, 4:].astype(f32) * slot_pair, axis=2)
    dots = jnp.stack(split(dots, 3), axis=-1)
    dots = jnp.pad(dots, ((0, 0), (4, 0), (0, 125)))
    block = jnp.concatenate([sums, dots], axis=2).reshape(16, half + 128)
    got = spread(block, ("x", "y"), 16).reshape(16, 2, 2, 4, half + 128)
    got = got.transpose(2, 1, 0, 3, 4).reshape(256, half + 128)
    back = lax.ppermute(got, "core", swap)
    rows = whole(got[:, :half], back[:, :half])
    slot_out, grad_slot_in = rows[:128], rows[128:]
    slot_dot = jnp.sum(
        got[128:, half : half + 3].astype(f32) + back[128:, half : half + 3].astype(f32),
        axis=1,
    )

    grad_comb = contract(slot_out, cotangent_t, 1, 0)
    grad_disp = contract(grad_slot_in, patches_t, 1, 0)
    patch_dot = jnp.sum(comb_prob * grad_comb, axis=0)
    grad_logits = disp_prob * (grad_disp - slot_dot[:, None]) + comb_prob * (
        grad_comb - patch_dot[None, :]
    )
    scaled = (grad_logits * scale).astype(bf16)

    own_scaled = lax.dynamic_slice_in_dim(scaled, 4 * expert, 4, 0)
    router_part = contract(own_scaled, patches_t, 1, 1)
    router_part = router_part + lax.ppermute(router_part, "core", swap)
    got = spread(router_part.astype(bf16).reshape(8, half), "zl", 8)
    grad_router = jnp.sum(got.astype(f32), axis=0).astype(bf16).reshape(4, width)

    def tokens(array):
        return lax.dynamic_slice_in_dim(array, 8 * expert, 8, 1)

    mixed = contract(tokens(combine), slot_out, 0, 0).astype(bf16)
    grad_patches = contract(tokens(dispatch), grad_slot_in, 0, 0) + contract(
        tokens(scaled), router_all, 0, 0
    )
    return (mixed, grad_patches.astype(bf16), grad_router, grad_w_in, grad_w_out)


def solution(mesh):
    fine = Mesh(mesh.devices.reshape(8, 2, 2, 4, 4), ("zl", "core", "zh", "x", "y"))
    tok, exp = ("zl", "core"), ("zh", "x", "y")
    return jax.shard_map(
        body,
        mesh=fine,
        in_specs=(
            P(tok, exp),
            P(exp, None),
            P(exp, tok, None),
            P(exp, tok, None),
            P(tok, exp),
        ),
        out_specs=(
            P(tok + exp, None),
            P(tok + exp, None),
            P(exp, None),
            P(exp, tok, None),
            P(exp, tok, None),
        ),
        check_vma=False,
    )
```

```python
import math

import jax
import jax.numpy as jnp
from jax import lax
from jax.experimental import pallas as pl
from jax.experimental.pallas import tpu as pltpu
from jax.sharding import Mesh, PartitionSpec as P

tanh_coef = 0.7978845608028654
cubic_coef = 0.044715
f32 = jnp.float32
bf16 = jnp.bfloat16
swap = [(0, 1), (1, 0)]


def gelu_value(inputs):
    return jax.nn.gelu(inputs, approximate=True)


def gelu_slope(inputs):
    inner = tanh_coef * (inputs + cubic_coef * inputs * inputs * inputs)
    hyper = jnp.tanh(inner)
    return 0.5 * (1.0 + hyper) + 0.5 * inputs * (1.0 - hyper * hyper) * tanh_coef * (
        1.0 + 3.0 * cubic_coef * inputs * inputs
    )


def contract(left, right, left_dim, right_dim):
    return lax.dot_general(
        left, right, (((left_dim,), (right_dim,)), ((), ())), preferred_element_type=f32
    )


def split(value, terms):
    out = []
    for _ in range(terms):
        head = lax.reduce_precision(value, 8, 7)
        out.append(head.astype(bf16))
        value = value - head
    return out


def spread(block, axes, count):
    return lax.all_to_all(
        jnp.broadcast_to(block[None], (count,) + block.shape), axes, 0, 0, tiled=True
    )


def fan_kernel(block_ref, out_ref):
    for peer in range(out_ref.shape[0]):
        out_ref[peer] = block_ref[...]


def fan(block, count, flops):
    return pl.pallas_call(
        fan_kernel,
        out_shape=jax.ShapeDtypeStruct((count,) + block.shape, block.dtype),
        in_specs=[pl.BlockSpec(memory_space=pltpu.VMEM)],
        out_specs=pl.BlockSpec(memory_space=pltpu.VMEM),
        compiler_params=pltpu.CompilerParams(vmem_limit_bytes=16 << 20),
        cost_estimate=pl.CostEstimate(flops=flops, bytes_accessed=0, transcendentals=0),
    )(block)


def body(patches, router, w_in, w_out, grad_mixed):
    core = lax.axis_index("core")
    expert = lax.axis_index(("zh", "x", "y"))
    low = core == 0
    width = router.shape[1]
    half = width // 2
    scale = 1.0 / math.sqrt(width)

    def mine(array):
        return jnp.where(low, array[:, :half], array[:, half:])

    def other(array):
        return jnp.where(low, array[:, half:], array[:, :half])

    def whole(own, got):
        return jnp.concatenate([jnp.where(low, own, got), jnp.where(low, got, own)], axis=1)

    packed = jnp.concatenate(
        [patches.T, grad_mixed.T] + [router[:, k * 256 : k * 256 + 256] for k in range(5)], axis=0
    )
    first = lax.axis_index("zh") == 0
    far = lax.all_to_all(fan(lax.ppermute(packed, "zh", swap), 16, 10**11), ("x", "y"), 0, 0, tiled=True)
    near = spread(packed, ("x", "y"), 16)

    def ordered(start, stop):
        own, partner = near[:, start:stop], far[:, start:stop]
        return jnp.stack([jnp.where(first, own, partner), jnp.where(first, partner, own)])

    patches_t = ordered(0, 40).reshape(width, 256)
    cotangent_t = ordered(40, 80).reshape(width, 256)
    router_all = (
        ordered(80, 100).reshape(32, 5, 4, 256).transpose(0, 2, 1, 3).reshape(128, width)
    )

    logits = contract(router_all, patches_t, 1, 0) * scale
    comb_exp = jnp.exp(logits - jnp.max(logits, axis=0, keepdims=True))
    comb_prob = comb_exp / jnp.sum(comb_exp, axis=0, keepdims=True)
    combine = comb_prob.astype(bf16)
    top = jnp.max(logits, axis=1)
    total = jnp.sum(jnp.exp(logits - top[:, None]), axis=1)

    stats = jnp.stack(split(top, 3) + split(total, 3))
    got = spread(jnp.pad(stats, ((0, 2), (0, 0))), ("zl", "core"), 16).astype(f32)
    tops = got[:, 0] + got[:, 1] + got[:, 2]
    slot_top = jnp.max(tops, axis=0)
    slot_sum = jnp.sum((got[:, 3] + got[:, 4] + got[:, 5]) * jnp.exp(tops - slot_top), axis=0)
    disp_prob = jnp.exp(logits - slot_top[:, None]) / slot_sum[:, None]
    dispatch, rest = split(disp_prob, 2)

    def own(array):
        return lax.dynamic_slice_in_dim(array, 4 * expert, 4, 0)

    parts = jnp.concatenate(
        [
            contract(jnp.concatenate([own(dispatch), own(rest)], axis=0), patches_t, 1, 1),
            contract(own(combine), cotangent_t, 1, 1),
        ],
        axis=0,
    )
    parts = mine(parts) + lax.ppermute(other(parts), "core", swap)
    block = jnp.concatenate(
        split(parts[:4], 2) + [parts[4:8].astype(bf16)] + split(parts[8:], 2), axis=0
    )
    got = jnp.sum(spread(block, "zl", 8).astype(f32), axis=0)
    slot_half = got[:4] + got[4:8]
    grad_half = got[12:16] + got[16:]
    halves = jnp.concatenate([slot_half, grad_half], axis=0).astype(bf16)

    rows = w_in.shape[1]
    in_own, in_far = mine(w_in[0]), lax.ppermute(other(w_in[0]), "core", swap)
    out_own, out_far = mine(w_out[0]), lax.ppermute(other(w_out[0]), "core", swap)

    def units(rows_of, own_part, far_part):
        return jnp.concatenate(
            [contract(rows_of, own_part, 1, 1), contract(rows_of, far_part, 1, 1)], axis=1
        )

    def features(units_of, own_part, far_part):
        return contract(units_of[:, :rows], own_part, 1, 0) + contract(
            units_of[:, rows:], far_part, 1, 0
        )

    pre = jnp.concatenate(
        [units(halves[:4], in_own, in_far), units(halves[4:], out_own, out_far)], axis=0
    )
    pre = pre + lax.ppermute(
        jnp.concatenate([pre[:, rows:], pre[:, :rows]], axis=1), "core", swap
    )
    pre_act, grad_hidden = pre[:4], pre[4:]
    hidden = gelu_value(pre_act).astype(bf16)
    grad_pre = (grad_hidden * gelu_slope(pre_act)).astype(bf16)
    parts = jnp.concatenate(
        [features(hidden, out_own, out_far), features(grad_pre, in_own, in_far)], axis=0
    )
    full = whole(halves, lax.ppermute(halves, "core", swap))
    grad_w_out = contract(hidden[:, :rows], full[4:], 0, 0).astype(bf16)[None]
    grad_w_in = contract(grad_pre[:, :rows], full[:4], 0, 0).astype(bf16)[None]

    piece = lax.dynamic_slice_in_dim(
        jnp.concatenate(split(slot_half + got[8:12], 2), axis=0), lax.axis_index("zl"), 1, 0
    )
    piece = jnp.pad(piece.reshape(5, 128), ((0, 3), (0, 0)))
    block = jnp.concatenate(split(parts, 2) + [piece], axis=1)
    got = spread(block, ("zh", "zl"), 16).reshape(2, 8, 8, width + 128)
    sums = jnp.sum(got[..., :width].astype(f32), axis=1)
    sums = (sums[..., :half] + sums[..., half:]).astype(bf16)
    pieces = got[:, :, :5, width:].reshape(2, 2, 4, half).astype(f32)
    slot_pair = pieces[:, 0] + pieces[:, 1]
    dots = jnp.sum(sums[:, 4:].astype(f32) * slot_pair, axis=2)
    dots = jnp.stack(split(dots, 3), axis=-1)
    dots = jnp.pad(dots, ((0, 0), (4, 0), (0, 125)))
    block = jnp.concatenate([sums, dots], axis=2).reshape(16, half + 128)
    got = spread(block, ("x", "y"), 16).reshape(16, 2, 2, 4, half + 128)
    got = got.transpose(2, 1, 0, 3, 4).reshape(256, half + 128)
    back = lax.ppermute(got, "core", swap)
    rows = whole(got[:, :half], back[:, :half])
    slot_out, grad_slot_in = rows[:128], rows[128:]
    slot_dot = jnp.sum(
        got[128:, half : half + 3].astype(f32) + back[128:, half : half + 3].astype(f32),
        axis=1,
    )

    grad_comb = contract(slot_out, cotangent_t, 1, 0)
    grad_disp = contract(grad_slot_in, patches_t, 1, 0)
    patch_dot = jnp.sum(comb_prob * grad_comb, axis=0)
    grad_logits = disp_prob * (grad_disp - slot_dot[:, None]) + comb_prob * (
        grad_comb - patch_dot[None, :]
    )
    scaled = (grad_logits * scale).astype(bf16)

    own_scaled = lax.dynamic_slice_in_dim(scaled, 4 * expert, 4, 0)
    router_part = contract(own_scaled, patches_t, 1, 1)
    router_part = router_part + lax.ppermute(router_part, "core", swap)
    got = spread(router_part.astype(bf16).reshape(8, half), "zl", 8)
    grad_router = jnp.sum(got.astype(f32), axis=0).astype(bf16).reshape(4, width)

    def tokens(array):
        return lax.dynamic_slice_in_dim(array, 8 * expert, 8, 1)

    mixed = contract(tokens(combine), slot_out, 0, 0).astype(bf16)
    grad_patches = contract(tokens(dispatch), grad_slot_in, 0, 0) + contract(
        tokens(scaled), router_all, 0, 0
    )
    return (mixed, grad_patches.astype(bf16), grad_router, grad_w_in, grad_w_out)


def solution(mesh):
    fine = Mesh(mesh.devices.reshape(8, 2, 2, 4, 4), ("zl", "core", "zh", "x", "y"))
    tok, exp = ("zl", "core"), ("zh", "x", "y")
    return jax.shard_map(
        body,
        mesh=fine,
        in_specs=(
            P(tok, exp),
            P(exp, None),
            P(exp, tok, None),
            P(exp, tok, None),
            P(tok, exp),
        ),
        out_specs=(
            P(tok + exp, None),
            P(tok + exp, None),
            P(exp, None),
            P(exp, tok, None),
            P(exp, tok, None),
        ),
        check_vma=False,
    )
```
